256 devices in a mesh: group: 4 (over x_lo, core), fsdp: 64 (over z, x_hi, y).
Axes of the slice: x: 4 (x_hi: 2, x_lo: 2; x = x_hi * 2 + x_lo), y: 4, z: 8, core: 2. Of those that a mesh axis runs over, the one named last changes fastest.
Arguments:
- tokens: bfloat16 [4, 128, 7168], P('group', 'fsdp'), may hold values from -6 to 6
- target: float32 [4, 128, 7168], P('group', 'fsdp'), may hold values from -6 to 6
- up_weight: bfloat16 [4, 10240, 7168], P('group', 'fsdp'), may hold values from -6 to 6
- down_weight: bfloat16 [4, 10240, 7168], P('group', 'fsdp'), may hold values from -6 to 6
Outputs:
- student_out: bfloat16 [4, 128, 7168], P('group', 'fsdp')
- new_up: bfloat16 [4, 10240, 7168], P('group', 'fsdp')
- new_down: bfloat16 [4, 10240, 7168], P('group', 'fsdp')
The draws below stay inside these ranges and needn't reach their ends.
All inputs are finite; a program needn't handle non-finite values.
Results may differ from the reference program's by a relative error of at most 0.0065.
Values may be sent and summed in bfloat16 or wider, within the bound.
A program may use at most 128 MiB of HBM per device.

```python
import math
import jax
import jax.numpy as jnp

D = 7168
FFW = 10240
TOKENS = 128
GROUPS = 4


def levels(rng, extent, shards, least, top_value):
    def one(dim, shards_of):
        steps = jax.random.uniform(jax.random.fold_in(jax.random.fold_in(rng, 6), dim), (shards_of,), jnp.float32, least / len(shards), top_value / len(shards))
        return jnp.repeat(jnp.exp(steps), extent[dim] // shards_of).reshape((-1,) + (1,) * (len(extent) - dim - 1))

    gain = one(*shards[0])
    for cut in shards[1:]:
        gain = gain * one(*cut)
    return gain


def centred(own_key, dims, scale, reach, pieces=(), held_as=jnp.bfloat16):
    factor_of = levels(own_key, dims, pieces, -0.22, 0.18) if pieces else 1.0
    array = jax.random.normal(own_key, dims, jnp.float32) * scale * factor_of
    return jnp.minimum(jnp.maximum(array, -reach), reach).astype(held_as)


def setup_inputs(seed: int = 0) -> dict:
    seeds = jax.random.split(jax.random.key(seed), 5)
    return {
        "tokens": centred(seeds[0], (GROUPS, TOKENS, D), 1.0, 6.0, ((0, 4), (1, 64))),
        "target": centred(seeds[1], (GROUPS, TOKENS, D), 1.0, 6.0, ((0, 4), (1, 64)), jnp.float32),
        "up_weight": centred(seeds[2], (GROUPS, FFW, D), 1.0, 6.0, ((0, 4), (1, 64))),
        "down_weight": centred(seeds[3], (GROUPS, FFW, D), 1.0, 6.0, ((0, 4), (1, 64))),
    }


def silu_parts(pre):
    sig = jax.nn.sigmoid(pre)
    return (pre * sig, sig * (1.0 + pre * (1.0 - sig)))

def forward(inputs, upper, lower):
    pre = jnp.dot(inputs, upper.T, preferred_element_type=jnp.float32) * (1.0 / math.sqrt(D))
    active, slope = silu_parts(pre)
    hidden = active.astype(jnp.bfloat16)
    result = jnp.dot(hidden, lower, preferred_element_type=jnp.float32) * (1.0 / math.sqrt(FFW))
    return (slope, hidden, result)

def reference(tokens, target, up_weight, down_weight):
    outs_list, ups, downs = ([], [], [])
    for group_id in range(GROUPS):
        inputs = tokens[group_id]
        partner = (group_id - 1) % GROUPS
        unused_a, unused_b, teacher = forward(inputs, up_weight[partner], down_weight[partner])
        upper, lower = (up_weight[group_id], down_weight[group_id])
        slope, hidden, student = forward(inputs, upper, lower)
        error = ((student - target[group_id] + (student - teacher)) * (1.0 / math.sqrt(TOKENS))).astype(jnp.bfloat16)
        grad_down = jnp.dot(hidden.T, error, preferred_element_type=jnp.float32) * (1.0 / math.sqrt(FFW))
        back = jnp.dot(error, lower.T, preferred_element_type=jnp.float32) * (1.0 / math.sqrt(FFW))
        dpre = (back * slope).astype(jnp.bfloat16)
        grad_up = jnp.dot(dpre.T, inputs, preferred_element_type=jnp.float32) * (1.0 / math.sqrt(D))
        outs_list.append(student.astype(jnp.bfloat16))
        ups.append((upper.astype(jnp.float32) - 32.0 * grad_up).astype(jnp.bfloat16))
        downs.append((lower.astype(jnp.float32) - 32.0 * grad_down).astype(jnp.bfloat16))
    return (jnp.stack(outs_list), jnp.stack(ups), jnp.stack(downs))
```

```python
import functools
import math

import jax
import jax.numpy as jnp
from jax import lax
from jax.experimental import pallas as pl
from jax.experimental.pallas import tpu as pltpu
from jax.sharding import PartitionSpec as P

MESH = pl.DeviceIdType.MESH
F32, BF16 = jnp.float32, jnp.bfloat16
D, FFW, TOKENS, HID = 7168, 10240, 128, 160
NZ, NP, ROWS = 8, 8, 16
HALF = D // 2
CHUNK = 1792
NCHUNK = D // CHUNK
UP_SCALE = 1.0 / math.sqrt(D)
DOWN_SCALE = 1.0 / math.sqrt(FFW)


def half(h):
    return pl.ds(h * HALF, HALF)


def kernel(
    tok, tgt, up_hbm, down_hbm, stu, nup_hbm, ndown_hbm,
    U, W, X, T, P1, P2, E, R, PB, EGB, EB, SB, RB, STK, load_sem, store_sem,
    pg_send, pg_recv, zg_send, zg_recv, tf_send, tf_recv,
    rs_send, rs_recv, pr_send, pr_recv, eg_send, eg_recv, ze_send, ze_recv,
):
    g = lax.axis_index("group")
    f = lax.axis_index("fsdp")
    z = f // NP
    me = f % NP
    base = z * NP
    below = (g + 3) % 4
    above = (g + 1) % 4
    up_z = ((z + 1) % NZ) * NP + me
    down_z = ((z + NZ - 1) % NZ) * NP + me
    ring = (up_z, down_z)
    flip = base + (me + 4) % NP
    other = jnp.where(g % 2 == 1, f, flip)

    load_up = pltpu.make_async_copy(up_hbm, U, load_sem.at[0])
    load_down = pltpu.make_async_copy(down_hbm, W, load_sem.at[1])
    load_up.start()
    load_down.start()

    barrier = pltpu.get_barrier_semaphore()
    for r in range(1, NP):
        pl.semaphore_signal(barrier, inc=1, device_id=(g, base + (me + r) % NP), device_id_type=MESH)
    for r in range(NP):
        pl.semaphore_signal(barrier, inc=1, device_id=(above, base + (me + r) % NP), device_id_type=MESH)
        pl.semaphore_signal(barrier, inc=1, device_id=(below, base + (me + r) % NP), device_id_type=MESH)
    for d in range(2):
        pl.semaphore_signal(barrier, inc=1, device_id=(g, ring[d]), device_id_type=MESH)
    pl.semaphore_wait(barrier, 3 * NP - 1 + 2)

    pending = []

    def plane_gather(src, buf, send, recv, slab):
        copies = []
        for r in range(1, NP):
            c = pltpu.make_async_remote_copy(
                src_ref=src, dst_ref=buf.at[me], send_sem=send.at[r], recv_sem=recv.at[r],
                device_id=(g, base + (me + r) % NP), device_id_type=MESH)
            c.start()
            copies.append(c)
        for c in copies:
            c.wait_recv()
        buf[me] = src[...]
        for j in range(NP):
            STK[2 * j:2 * j + 2, :] = buf[j].astype(F32)
        slab[...] = STK[...].astype(BF16)
        pending.extend(copies)

    def ring_gather(buf, send, recv, forward=None):
        def send_slab(d, s, h):
            slab = (z + s) % NZ if d == 1 else (z + NZ - s) % NZ
            c = pltpu.make_async_remote_copy(
                src_ref=buf.at[slab, :, half(h)], dst_ref=buf.at[slab, :, half(h)],
                send_sem=send.at[d, s, h], recv_sem=recv.at[d, s, h],
                device_id=(g, ring[d]), device_id_type=MESH)
            c.start()
            pending.append(c)
            return c

        flight = {}
        for h in range(2):
            for d in range(2):
                flight[d, 0, h] = send_slab(d, 0, h)
        if forward is not None:
            forward(z, 0, 0)
            forward(z, 0, 1)
        for s in range(1, 5):
            for h in range(2):
                for d in range(2):
                    if (d, s - 1, h) not in flight:
                        continue
                    flight[d, s - 1, h].wait_recv()
                    if s < 3 or (s == 3 and h == d):
                        flight[d, s, h] = send_slab(d, s, h)
                    if forward is not None:
                        got = (z + s) % NZ if d == 1 else (z + NZ - s) % NZ
                        forward(got, s if d == 0 else (s + 4 if s < 4 else 4), h)

    sent_t = []

    def forward(slab, slot, h):
        dev = f if h == 0 else other
        c = pltpu.make_async_remote_copy(
            src_ref=X.at[slab, :, half(h)], dst_ref=T.at[slab, :, half(h)],
            send_sem=tf_send.at[slot, h], recv_sem=tf_recv.at[slot, h],
            device_id=(below, dev), device_id_type=MESH)
        c.start()
        sent_t.append(c)

    plane_gather(tok, PB, pg_send, pg_recv, X.at[z])
    ring_gather(X, zg_send, zg_recv, forward)

    load_up.wait()
    load_down.wait()

    def pre_of(A):
        def body(i, acc):
            cols = pl.ds(pl.multiple_of(i * CHUNK, CHUNK), CHUNK)
            a = A[:, :, cols].reshape(TOKENS, CHUNK)
            return acc + lax.dot_general(
                a, U[:, cols], (((1,), (1,)), ((), ())), preferred_element_type=F32)
        return lax.fori_loop(0, NCHUNK, body, jnp.zeros((TOKENS, HID), F32)) * UP_SCALE

    def partial_out(hidden, out):
        def body(i, _):
            cols = pl.ds(pl.multiple_of(i * CHUNK, CHUNK), CHUNK)
            v = jnp.dot(hidden, W[:, cols], preferred_element_type=F32) * DOWN_SCALE
            out[:, :, cols] = v.astype(BF16).reshape(NZ, ROWS, CHUNK)
            return 0
        lax.fori_loop(0, NCHUNK, body, 0)

    rflight = {}

    def rs_start(w, part):
        for d in range(2):
            c = pltpu.make_async_remote_copy(
                src_ref=part.at[(z + 4) % NZ, :, half(d)], dst_ref=R.at[w, d, 0, :, half(d)],
                send_sem=rs_send.at[w, d, 0, d], recv_sem=rs_recv.at[w, d, 0, d],
                device_id=(g, ring[d]), device_id_type=MESH)
            c.start()
            rflight[w, d, 0, d] = c
        for d in range(2):
            dest = (z + 3) % NZ if d == 0 else (z + NZ - 3) % NZ
            h = 1 - d
            c = pltpu.make_async_remote_copy(
                src_ref=part.at[dest, :, half(h)], dst_ref=R.at[w, d, 1, :, half(h)],
                send_sem=rs_send.at[w, d, 1, h], recv_sem=rs_recv.at[w, d, 1, h],
                device_id=(g, ring[d]), device_id_type=MESH)
            c.start()
            rflight[w, d, 1, h] = c

    def rs_step(w, part, s):
        for h in range(2):
            for d in range(2):
                if (w, d, s - 1, h) not in rflight:
                    continue
                rflight[w, d, s - 1, h].wait_recv()
                dest = (z + 4 - s) % NZ if d == 0 else (z + NZ - 4 + s) % NZ
                cols = half(h)
                R[w, d, s - 1, :, cols] = (
                    R[w, d, s - 1, :, cols].astype(F32) + part[dest, :, cols].astype(F32)
                ).astype(BF16)
                c = pltpu.make_async_remote_copy(
                    src_ref=R.at[w, d, s - 1, :, cols], dst_ref=R.at[w, d, s, :, cols],
                    send_sem=rs_send.at[w, d, s, h], recv_sem=rs_recv.at[w, d, s, h],
                    device_id=(g, ring[d]), device_id_type=MESH)
                c.start()
                rflight[w, d, s, h] = c

    pr = []

    def rs_finish(w, part):
        for h in range(2):
            for d in range(2):
                rflight[w, d, 3, h].wait_recv()
        total = part[z].astype(F32) + R[w, 0, 3].astype(F32) + R[w, 1, 3].astype(F32)
        STK[...] = total
        for j in range(NP):
            SB[w, j] = STK[2 * j:2 * j + 2, :].astype(BF16)
        for r in range(NP):
            if w == 0 and r == 0:
                continue
            peer = (me + r) % NP
            c = pltpu.make_async_remote_copy(
                src_ref=SB.at[w, peer], dst_ref=RB.at[w, me],
                send_sem=pr_send.at[w, r], recv_sem=pr_recv.at[w, r],
                device_id=(g if w == 0 else above, base + peer), device_id_type=MESH)
            c.start()
            pr.append(c)
        if w == 0:
            RB[w, me] = SB[w, me]

    pre = pre_of(X)
    sig = jax.nn.sigmoid(pre)
    hidden = (pre * sig).astype(BF16)
    slope = sig * (1.0 + pre * (1.0 - sig))
    partial_out(hidden, P1)
    rs_start(0, P1)
    for c in sent_t:
        c.wait_recv()
    pre_t = pre_of(T)
    hidden_t = (pre_t * jax.nn.sigmoid(pre_t)).astype(BF16)
    partial_out(hidden_t, P2)
    rs_start(1, P2)
    parts = (P1, P2)
    for s in range(1, 4):
        for w in range(2):
            rs_step(w, parts[w], s)
    for w in range(2):
        rs_finish(w, parts[w])
    for c in pr:
        c.wait_recv()
    ys = jnp.sum(RB[0].astype(F32), axis=0)
    yt = jnp.sum(RB[1].astype(F32), axis=0)
    stu[...] = ys.astype(BF16)
    EB[...] = ((ys - tgt[...] + (ys - yt)) * (1.0 / math.sqrt(TOKENS))).astype(BF16)

    plane_gather(EB, EGB, eg_send, eg_recv, E.at[z])
    ring_gather(E, ze_send, ze_recv)

    hidden_t_up = jnp.transpose(hidden.astype(F32)).astype(BF16)

    def back_body(i, acc):
        cols = pl.ds(pl.multiple_of(i * CHUNK, CHUNK), CHUNK)
        e = E[:, :, cols].reshape(TOKENS, CHUNK)
        w = W[:, cols]
        acc = acc + lax.dot_general(
            e, w, (((1,), (1,)), ((), ())), preferred_element_type=F32)
        grad = jnp.dot(hidden_t_up, e, preferred_element_type=F32) * DOWN_SCALE
        W[:, cols] = (w.astype(F32) - 32.0 * grad).astype(BF16)
        return acc

    back = lax.fori_loop(0, NCHUNK, back_body, jnp.zeros((TOKENS, HID), F32)) * DOWN_SCALE
    store_down = pltpu.make_async_copy(W, ndown_hbm, store_sem.at[0])
    store_down.start()
    dpre_t = jnp.transpose(back * slope).astype(BF16)

    def up_body(i, _):
        cols = pl.ds(pl.multiple_of(i * CHUNK, CHUNK), CHUNK)
        x = X[:, :, cols].reshape(TOKENS, CHUNK)
        grad = jnp.dot(dpre_t, x, preferred_element_type=F32) * UP_SCALE
        U[:, cols] = (U[:, cols].astype(F32) - 32.0 * grad).astype(BF16)
        return 0

    lax.fori_loop(0, NCHUNK, up_body, 0)
    store_up = pltpu.make_async_copy(U, nup_hbm, store_sem.at[1])
    store_up.start()
    for c in pending + sent_t + pr + list(rflight.values()):
        c.wait_send()
    store_down.wait()
    store_up.wait()


def shards(tokens, target, up_weight, down_weight):
    anywhere = pl.BlockSpec(memory_space=pl.ANY)
    vmem = pl.BlockSpec(memory_space=pltpu.VMEM)
    dma = pltpu.SemaphoreType.DMA
    student, new_up, new_down = pl.pallas_call(
        kernel,
        out_shape=(
            jax.ShapeDtypeStruct((2, D), BF16),
            jax.ShapeDtypeStruct((HID, D), BF16),
            jax.ShapeDtypeStruct((HID, D), BF16),
        ),
        in_specs=[vmem, vmem, anywhere, anywhere],
        out_specs=(vmem, anywhere, anywhere),
        scratch_shapes=[
            pltpu.VMEM((HID, D), BF16),
            pltpu.VMEM((HID, D), BF16),
            pltpu.VMEM((NZ, ROWS, D), BF16),
            pltpu.VMEM((NZ, ROWS, D), BF16),
            pltpu.VMEM((NZ, ROWS, D), BF16),
            pltpu.VMEM((NZ, ROWS, D), BF16),
            pltpu.VMEM((NZ, ROWS, D), BF16),
            pltpu.VMEM((2, 2, 4, ROWS, D), BF16),
            pltpu.VMEM((NP, 2, D), BF16),
            pltpu.VMEM((NP, 2, D), BF16),
            pltpu.VMEM((2, D), BF16),
            pltpu.VMEM((2, NP, 2, D), BF16),
            pltpu.VMEM((2, NP, 2, D), BF16),
            pltpu.VMEM((ROWS, D), F32),
            dma((2,)), dma((2,)),
            dma((NP,)), dma((NP,)),
            dma((2, 4, 2)), dma((2, 4, 2)),
            dma((8, 2)), dma((8, 2)),
            dma((2, 2, 4, 2)), dma((2, 2, 4, 2)),
            dma((2, NP)), dma((2, NP)),
            dma((NP,)), dma((NP,)),
            dma((2, 4, 2)), dma((2, 4, 2)),
        ],
        compiler_params=pltpu.CompilerParams(
            collective_id=0, has_side_effects=True, vmem_limit_bytes=48 * 1024 * 1024),
        cost_estimate=pl.CostEstimate(
            flops=14 * TOKENS * HID * D, bytes_accessed=8 * HID * D, transcendentals=2 * TOKENS * HID),
        name="codistill",
    )(tokens[0], target[0], up_weight[0], down_weight[0])
    return student[None], new_up[None], new_down[None]


def solution(mesh):
    placed = P("group", "fsdp", None)
    return jax.shard_map(
        shards, mesh=mesh, in_specs=(placed,) * 4, out_specs=(placed,) * 3, check_vma=False)
```

```python
import math

import jax
import jax.numpy as jnp
from jax import lax
from jax.experimental import pallas as pl
from jax.experimental.pallas import tpu as pltpu
from jax.sharding import PartitionSpec as P

MESH = pl.DeviceIdType.MESH
F32, BF16 = jnp.float32, jnp.bfloat16
D, FFW, TOKENS, HID = 7168, 10240, 128, 160
NZ, NP, NY, ROWS = 8, 8, 4, 16
CA = 3072
CB = D - CA
HA, HB = CA // 2, CB // 2
UP_SCALE = 1.0 / math.sqrt(D)
DOWN_SCALE = 1.0 / math.sqrt(FFW)

SCRATCH = {}


def scratch(name, shape, kind=BF16):
    SCRATCH[name] = pltpu.SemaphoreType.DMA(shape) if kind is None else pltpu.VMEM(shape, kind)


scratch("tok", (2, D))
scratch("tgt", (2, D), F32)
scratch("U", (HID, D))
scratch("W", (HID, D))
for n in ("X", "T", "P1", "P2", "E"):
    scratch(n + "a", (NZ, ROWS, CA))
    scratch(n + "b", (NP, ROWS, CB))
scratch("RA", (2, 2, 4, ROWS, CA))
scratch("RY", (2, 2, 2, 2, ROWS, CB))
scratch("XS", (2, ROWS, CB))
scratch("XR", (2, ROWS, CB))
scratch("err", (2, D))
for n in ("G1", "G2"):
    scratch(n + "a", (NP, 2, CA))
    scratch(n + "b", (NZ, 2, CB))
for n in ("S", "R"):
    scratch(n + "Pa", (2, NP, 2, CA))
    scratch(n + "Pb", (2, NZ, 2, CB))
scratch("STKa", (ROWS, CA), F32)
scratch("STKb", (ROWS, CB), F32)
scratch("load", (4,), None)
scratch("store", (2,), None)
for n in ("g1", "g2"):
    for e in ("s", "r"):
        scratch(n + "pa" + e, (NP,), None)
        scratch(n + "pb" + e, (NZ,), None)
        scratch(n + "za" + e, (2, 4, 2), None)
        scratch(n + "xb" + e, (2,), None)
        scratch(n + "yb" + e, (2, 2, 2, 2), None)
for e in ("s", "r"):
    scratch("ta" + e, (NZ, 2), None)
    scratch("tb" + e, (NP, 2), None)
    scratch("ra" + e, (2, 2, 4, 2), None)
    scratch("ry" + e, (2, 2, 2, 2, 2), None)
    scratch("rx" + e, (2, 2), None)
    scratch("pa" + e, (2, NP), None)
    scratch("pb" + e, (2, NZ), None)


def kernel(tok_hbm, tgt_hbm, up_hbm, down_hbm, stu, nup_hbm, ndown_hbm, *refs):
    v = dict(zip(SCRATCH, refs))
    tok, U, W = v["tok"], v["U"], v["W"]
    g = lax.axis_index("group")
    f = lax.axis_index("fsdp")
    z = f // NP
    me = f % NP
    xh = me // NY
    yy = me % NY
    base = z * NP
    below = (g + 3) % 4
    above = (g + 1) % 4
    zring = (((z + 1) % NZ) * NP + me, ((z + NZ - 1) % NZ) * NP + me)
    yring = (base + xh * NY + (yy + 1) % NY, base + xh * NY + (yy + NY - 1) % NY)
    flip = base + (me + 4) % NP
    other = jnp.where(g % 2 == 1, f, flip)

    def colsa(h):
        return pl.ds(h * HA, HA)

    def colsb(h):
        return pl.ds(h * HB, HB)

    loads = [
        pltpu.make_async_copy(src, dst, v["load"].at[i])
        for i, (src, dst) in enumerate(
            ((tok_hbm, tok), (up_hbm, U), (down_hbm, W), (tgt_hbm, v["tgt"])))
    ]
    for c in loads:
        c.start()

    barrier = pltpu.get_barrier_semaphore()
    peers = [(g, base + (me + r) % NP) for r in range(1, NP)]
    peers += [(g, ((z + r) % NZ) * NP + me) for r in range(1, NZ)]
    peers += [(above, f), (above, flip), (below, f), (below, flip)]
    for p in peers:
        pl.semaphore_signal(barrier, inc=1, device_id=p, device_id_type=MESH)
    pl.semaphore_wait(barrier, len(peers))

    started = []

    def send(src, dst, sems, at, dev):
        c = pltpu.make_async_remote_copy(
            src_ref=src, dst_ref=dst, send_sem=v[sems + "s"].at[at], recv_sem=v[sems + "r"].at[at],
            device_id=dev, device_id_type=MESH)
        c.start()
        started.append(c)
        return c

    def slab_of(p, k, s):
        x = xh if k == 0 else 1 - xh
        return x * NY + (yy + s + NY) % NY

    def stack(buf, stk, slab):
        for j in range(8):
            stk[2 * j:2 * j + 2, :] = buf[j].astype(F32)
        slab[...] = stk[...].astype(BF16)

    def gather(src, n, name, forward):
        Ga, Gb = v[n.upper() + "a"], v[n.upper() + "b"]
        A, B = v[name + "a"], v[name + "b"]
        first_a = [
            send(src.at[:, pl.ds(0, CA)], Ga.at[me], n + "pa", (r,), (g, base + (me + r) % NP))
            for r in range(1, NP)]
        first_b = [
            send(src.at[:, pl.ds(CA, CB)], Gb.at[z], n + "pb", (r,), (g, ((z + r) % NZ) * NP + me))
            for r in range(1, NZ)]
        Ga[me] = src[:, 0:CA]
        Gb[z] = src[:, CA:D]
        fly = {}

        def send_a(d, s, h):
            at = (z + s) % NZ if d == 1 else (z + NZ - s) % NZ
            ref = A.at[at, :, colsa(h)]
            fly["a", d, s, h] = send(ref, ref, n + "za", (d, s, h), (g, zring[d]))

        def step_a(s):
            for h in range(2):
                for d in range(2):
                    if ("a", d, s - 1, h) not in fly:
                        continue
                    fly["a", d, s - 1, h].wait_recv()
                    if s < 3 or (s == 3 and h == d):
                        send_a(d, s, h)
                    if forward:
                        at = (z + s) % NZ if d == 1 else (z + NZ - s) % NZ
                        forward("a", at, s if d == 0 else (s + 4 if s < 4 else 4), h)

        def send_b(d, k, s, h):
            at = slab_of(me, k, s if d == 1 else -s)
            ref = B.at[at, :, colsb(h)]
            fly["b", d, k, s, h] = send(ref, ref, n + "yb", (d, k, s, h), (g, yring[d]))

        def step_b(k, s):
            for h in range(2):
                for d in range(2):
                    if ("b", d, k, s - 1, h) not in fly:
                        continue
                    fly["b", d, k, s - 1, h].wait_recv()
                    if s == 1 and h == d:
                        send_b(d, k, 1, h)
                    if forward:
                        at = slab_of(me, k, s if d == 1 else -s)
                        slot = 4 * k + (s if d == 0 else (3 if s == 1 else 2))
                        forward("b", at, slot, h)

        for c in first_a:
            c.wait_recv()
        stack(Ga, v["STKa"], A.at[z])
        for h in range(2):
            for d in range(2):
                send_a(d, 0, h)
        for c in first_b:
            c.wait_recv()
        stack(Gb, v["STKb"], B.at[me])
        for h in range(2):
            ref = B.at[me, :, colsb(h)]
            fly["x", h] = send(ref, ref, n + "xb", (h,), (g, flip))
            for d in range(2):
                send_b(d, 0, 0, h)
        if forward:
            for h in range(2):
                forward("a", z, 0, h)
                forward("b", me, 0, h)
        step_a(1)
        for h in range(2):
            fly["x", h].wait_recv()
            for d in range(2):
                send_b(d, 1, 0, h)
            if forward:
                forward("b", slab_of(me, 1, 0), 4, h)
        step_b(0, 1)
        step_a(2)
        step_b(1, 1)
        step_a(3)
        step_b(0, 2)
        step_a(4)
        step_b(1, 2)

    sent_t = []

    def forward(o, slab, slot, h):
        cols = colsa(h) if o == "a" else colsb(h)
        sent_t.append(send(
            v["X" + o].at[slab, :, cols], v["T" + o].at[slab, :, cols], "t" + o, (slot, h),
            (below, f if h == 0 else other)))

    loads[0].wait()
    gather(tok, "g1", "X", forward)
    loads[1].wait()
    loads[2].wait()
    loads[3].wait()

    row = lax.broadcasted_iota(jnp.int32, (TOKENS, TOKENS), 0)
    col = lax.broadcasted_iota(jnp.int32, (TOKENS, TOKENS), 1)
    mirrored = (row // 2 % 8) * 16 + (row // 16) * 2 + row % 2
    swap = (mirrored == col).astype(F32)
    swap_bf = swap.astype(BF16)

    def swapped(x):
        return jnp.dot(swap, x, preferred_element_type=F32, precision=lax.Precision.HIGHEST)

    def swapped_bf(x):
        return jnp.dot(swap_bf, x, preferred_element_type=F32).astype(BF16)

    def contract(A, M, first, width):
        def body(i, acc):
            at = pl.multiple_of(i * width, width)
            a = A[:, :, pl.ds(at, width)].reshape(TOKENS, width)
            m = M[:, pl.ds(first + at, width)]
            return acc + lax.dot_general(
                a, m, (((1,), (1,)), ((), ())), preferred_element_type=F32)
        return lax.fori_loop(0, 2, body, jnp.zeros((TOKENS, HID), F32))

    def expand(hidden, out, first, width):
        def body(i, _):
            at = pl.multiple_of(i * width, width)
            y = jnp.dot(hidden, W[:, pl.ds(first + at, width)], preferred_element_type=F32)
            out[:, :, pl.ds(at, width)] = (y * DOWN_SCALE).astype(BF16).reshape(8, ROWS, width)
            return 0
        lax.fori_loop(0, 2, body, 0)

    fly = {}
    RA, RY = v["RA"], v["RY"]

    def rsa_send(w, src, d, s, h):
        fly["a", w, d, s, h] = send(
            src, RA.at[w, d, s, :, colsa(h)], "ra", (w, d, s, h), (g, zring[d]))

    def rsa_start(w, part):
        for d in range(2):
            rsa_send(w, part.at[(z + 4) % NZ, :, colsa(d)], d, 0, d)
        for d in range(2):
            dest = (z + 3) % NZ if d == 0 else (z + NZ - 3) % NZ
            rsa_send(w, part.at[dest, :, colsa(1 - d)], d, 1, 1 - d)

    def rsa_step(w, part, s):
        for h in range(2):
            for d in range(2):
                if ("a", w, d, s - 1, h) not in fly:
                    continue
                fly["a", w, d, s - 1, h].wait_recv()
                dest = (z + 4 - s) % NZ if d == 0 else (z + NZ - 4 + s) % NZ
                held = RA.at[w, d, s - 1, :, colsa(h)]
                held[...] = (
                    held[...].astype(F32) + part[dest, :, colsa(h)].astype(F32)).astype(BF16)
                rsa_send(w, held, d, s, h)

    def rsy_send(w, src, d, k, s, h):
        fly["b", w, d, k, s, h] = send(
            src, RY.at[w, d, k, s, :, colsb(h)], "ry", (w, d, k, s, h), (g, yring[d]))

    def rsb_start(w, part):
        for k in (1, 0):
            for d in range(2):
                rsy_send(w, part.at[slab_of(me, k, 2), :, colsb(d)], d, k, 0, d)
        for k in (1, 0):
            for d in range(2):
                dest = slab_of(me, k, 1 if d == 0 else -1)
                rsy_send(w, part.at[dest, :, colsb(1 - d)], d, k, 1, 1 - d)

    def rsb_step(w, part, k):
        for d in range(2):
            fly["b", w, d, k, 0, d].wait_recv()
            dest = slab_of(me, k, 1 if d == 0 else -1)
            held = RY.at[w, d, k, 0, :, colsb(d)]
            held[...] = (
                held[...].astype(F32) + part[dest, :, colsb(d)].astype(F32)).astype(BF16)
            rsy_send(w, held, d, k, 1, d)

    def rsb_sum(w, part, k, h):
        for d in range(2):
            fly["b", w, d, k, 1, h].wait_recv()
        cols = colsb(h)
        return (
            part[slab_of(me, k, 0), :, cols].astype(F32)
            + RY[w, 0, k, 1, :, cols].astype(F32) + RY[w, 1, k, 1, :, cols].astype(F32))

    def rsb_cross(w, part):
        for h in range(2):
            cols = colsb(h)
            v["XS"][w, :, cols] = rsb_sum(w, part, 1, h).astype(BF16)
            fly["x", w, h] = send(
                v["XS"].at[w, :, cols], v["XR"].at[w, :, cols], "rx", (w, h), (g, flip))

    last = []

    def pieces(w, o, mine, device):
        S, R, stk = v["SP" + o], v["RP" + o], v["STK" + o]
        for j in range(8):
            S[w, j] = stk[2 * j:2 * j + 2, :].astype(BF16)
        for r in range(8):
            if w == 0 and r == 0:
                continue
            to = (mine + r) % 8
            last.append(send(
                S.at[w, to], R.at[w, mine], "p" + o, (w, r), (g if w == 0 else above, device(to))))
        if w == 0:
            R[w, mine] = S[w, mine]

    def rsb_finish(w, part):
        for h in range(2):
            own = rsb_sum(w, part, 0, h)
            fly["x", w, h].wait_recv()
            v["STKb"][:, h * HB:(h + 1) * HB] = own + v["XR"][w, :, colsb(h)].astype(F32)
        pieces(w, "b", z, lambda j: j * NP + me)

    def rsa_finish(w, part):
        for h in range(2):
            for d in range(2):
                fly["a", w, d, 3, h].wait_recv()
        v["STKa"][...] = (
            part[z].astype(F32) + RA[w, 0, 3].astype(F32) + RA[w, 1, 3].astype(F32))
        pieces(w, "a", me, lambda j: base + j)

    pre = (contract(v["Xa"], U, 0, HA) + swapped(contract(v["Xb"], U, CA, HB))) * UP_SCALE
    sig = jax.nn.sigmoid(pre)
    hidden = (pre * sig).astype(BF16)
    hidden_b = swapped_bf(hidden)
    slope = sig * (1.0 + pre * (1.0 - sig))
    expand(hidden, v["P1a"], 0, HA)
    rsa_start(0, v["P1a"])
    expand(hidden_b, v["P1b"], CA, HB)
    rsb_start(0, v["P1b"])
    for c in sent_t:
        c.wait_recv()
    pre_t = (contract(v["Ta"], U, 0, HA) + swapped(contract(v["Tb"], U, CA, HB))) * UP_SCALE
    hidden_t = (pre_t * jax.nn.sigmoid(pre_t)).astype(BF16)
    expand(hidden_t, v["P2a"], 0, HA)
    rsa_start(1, v["P2a"])
    expand(swapped_bf(hidden_t), v["P2b"], CA, HB)
    rsb_start(1, v["P2b"])
    Pa, Pb = (v["P1a"], v["P2a"]), (v["P1b"], v["P2b"])
    rsa_step(0, Pa[0], 1)
    rsb_step(0, Pb[0], 1)
    rsb_step(0, Pb[0], 0)
    rsa_step(1, Pa[1], 1)
    rsb_step(1, Pb[1], 1)
    rsb_step(1, Pb[1], 0)
    rsa_step(0, Pa[0], 2)
    rsb_cross(0, Pb[0])
    rsa_step(1, Pa[1], 2)
    rsb_cross(1, Pb[1])
    rsa_step(0, Pa[0], 3)
    rsb_finish(0, Pb[0])
    rsa_step(1, Pa[1], 3)
    rsb_finish(1, Pb[1])
    rsa_finish(0, Pa[0])
    rsa_finish(1, Pa[1])
    for c in last:
        c.wait_recv()
    for o, first, count in (("a", 0, CA), ("b", CA, CB)):
        ys = jnp.sum(v["RP" + o][0].astype(F32), axis=0)
        yt = jnp.sum(v["RP" + o][1].astype(F32), axis=0)
        goal = v["tgt"][:, first:first + count]
        stu[:, first:first + count] = ys.astype(BF16)
        v["err"][:, first:first + count] = (
            (ys - goal + (ys - yt)) * (1.0 / math.sqrt(TOKENS))).astype(BF16)

    gather(v["err"], "g2", "E", None)

    def downs(rows, E, first, width):
        def body(i, acc):
            at = pl.multiple_of(i * width, width)
            e = E[:, :, pl.ds(at, width)].reshape(TOKENS, width)
            m = W[:, pl.ds(first + at, width)]
            grad = jnp.dot(rows, e, preferred_element_type=F32) * DOWN_SCALE
            W[:, pl.ds(first + at, width)] = (m.astype(F32) - 32.0 * grad).astype(BF16)
            return acc + lax.dot_general(
                e, m, (((1,), (1,)), ((), ())), preferred_element_type=F32)
        return lax.fori_loop(0, 2, body, jnp.zeros((TOKENS, HID), F32))

    def ups(rows, X, first, width):
        def body(i, _):
            at = pl.multiple_of(i * width, width)
            x = X[:, :, pl.ds(at, width)].reshape(TOKENS, width)
            grad = jnp.dot(rows, x, preferred_element_type=F32) * UP_SCALE
            cols = pl.ds(first + at, width)
            U[:, cols] = (U[:, cols].astype(F32) - 32.0 * grad).astype(BF16)
            return 0
        lax.fori_loop(0, 2, body, 0)

    def turned(x):
        return jnp.transpose(x.astype(F32)).astype(BF16)

    back = downs(turned(hidden), v["Ea"], 0, HA) + swapped(downs(turned(hidden_b), v["Eb"], CA, HB))
    store_down = pltpu.make_async_copy(W, ndown_hbm, v["store"].at[0])
    store_down.start()
    dpre = (back * DOWN_SCALE * slope).astype(BF16)
    ups(turned(dpre), v["Xa"], 0, HA)
    ups(turned(swapped_bf(dpre)), v["Xb"], CA, HB)
    store_up = pltpu.make_async_copy(U, nup_hbm, v["store"].at[1])
    store_up.start()
    for c in started:
        c.wait_send()
    store_down.wait()
    store_up.wait()


def shards(tokens, target, up_weight, down_weight):
    anywhere = pl.BlockSpec(memory_space=pl.ANY)
    student, new_up, new_down = pl.pallas_call(
        kernel,
        out_shape=(
            jax.ShapeDtypeStruct((2, D), BF16),
            jax.ShapeDtypeStruct((HID, D), BF16),
            jax.ShapeDtypeStruct((HID, D), BF16),
        ),
        in_specs=[anywhere] * 4,
        out_specs=(pl.BlockSpec(memory_space=pltpu.VMEM), anywhere, anywhere),
        scratch_shapes=list(SCRATCH.values()),
        compiler_params=pltpu.CompilerParams(
            collective_id=0, has_side_effects=True, vmem_limit_bytes=48 * 1024 * 1024),
        cost_estimate=pl.CostEstimate(
            flops=14 * TOKENS * HID * D, bytes_accessed=8 * HID * D, transcendentals=2 * TOKENS * HID),
        name="codistill",
    )(tokens[0], target[0], up_weight[0], down_weight[0])
    return student[None], new_up[None], new_down[None]


def solution(mesh):
    placed = P("group", "fsdp", None)
    return jax.shard_map(
        shards, mesh=mesh, in_specs=(placed,) * 4, out_specs=(placed,) * 3, check_vma=False)
```
